32 devices in a mesh: chan: 2 (over y), tile: 16 (over z, x, core).
Axes of the slice: x: 2, y: 2, z: 4, core: 2. Of those that a mesh axis runs over, the one named last changes fastest.
Arguments:
- image: bfloat16 [256, 256, 256], P('chan', 'tile'), may hold values from -6 to 6
- w_down: bfloat16 [2, 2, 256, 512], P(None, None, None, 'chan'), may hold values from -0.1875 to 0.1875
- w_mix: bfloat16 [3, 3, 512, 512], P(None, None, None, 'chan'), may hold values from -0.09375 to 0.09375
- cotangent: bfloat16 [512, 128, 128], P('chan', 'tile'), may hold values from -6 to 6
Outputs:
- mixed: bfloat16 [512, 128, 128], P('chan', 'tile')
- grad_mix: float32 [512, 3, 3, 512], P('tile', None, None, 'chan')
- grad_down: float32 [256, 2, 2, 512], P('tile', None, None, 'chan')
- grad_image: bfloat16 [256, 256, 256], P('chan', 'tile')
The draws below stay inside these ranges and needn't reach their ends.
All inputs are finite; a program needn't handle non-finite values.
Results may differ from the reference program's by a relative error of at most 0.0049.
Values may be sent and summed in bfloat16 or wider, within the bound.
A program may use at most 64 MiB of HBM per device.

```python
import math
import jax
import jax.numpy as jnp

C0 = 256
C1 = 512
COLS = 128
OUT_ROWS = 128


def levels(own_key, dims, cuts, low, top_value):
    gain = 1.0
    for axis_at, shards_of in cuts:
        draws = jax.random.uniform(jax.random.fold_in(jax.random.fold_in(own_key, 6), axis_at), (shards_of,), jnp.float32, low / len(cuts), top_value / len(cuts))
        gain = gain * jnp.repeat(jnp.exp(draws), dims[axis_at] // shards_of).reshape((-1,) + (1,) * (len(dims) - 1 - axis_at))
    return gain


def bell_draw(stream_key, extent, deviation, reach, cuts=(), held_as=jnp.bfloat16):
    gain = levels(stream_key, extent, cuts, -0.22, 0.18) if cuts else 1.0
    array = jax.random.normal(stream_key, extent, jnp.float32) * deviation * gain
    return jnp.minimum(jnp.maximum(array, -reach), reach).astype(held_as)


def setup_inputs(seed: int = 0) -> dict:
    key_of = jax.random.split(jax.random.key(seed), 5)
    image = bell_draw(key_of[0], (C0, 2 * OUT_ROWS, 2 * COLS), 1.0, 6.0, ((0, 2), (1, 16)))
    w_down = bell_draw(key_of[1], (2, 2, C0, C1), (4 * C0) ** -0.5, 0.1875, ((3, 2),))
    w_mix = bell_draw(key_of[2], (3, 3, C1, C1), (9 * C1) ** -0.5, 0.09375, ((3, 2),))
    cotangent = bell_draw(key_of[3], (C1, OUT_ROWS, COLS), 1.0, 6.0, ((0, 2), (1, 16)))
    return dict(image=image, w_down=w_down, w_mix=w_mix, cotangent=cotangent)


def normal_cdf(value):
    return 0.5 * (1.0 + jax.scipy.special.erf(value / math.sqrt(2.0)))

def normal_pdf(value):
    return jnp.exp(-0.5 * value * value) / math.sqrt(2.0 * math.pi)

def reference(image, w_down, w_mix, cotangent):
    in_chan, in_rows, in_cols = image.shape
    n_rows = in_rows // 2
    n_cols = in_cols // 2
    scale = 1.0 / math.sqrt(n_rows * n_cols)
    patches = image.astype(jnp.float32).reshape(in_chan, n_rows, 2, n_cols, 2)
    down32 = w_down.astype(jnp.float32)
    mix32 = w_mix.astype(jnp.float32)
    preact = jnp.einsum('crawb,abcd->drw', patches, down32)
    hidden = (preact * normal_cdf(preact)).astype(jnp.bfloat16)
    hidden_pad = jnp.pad(hidden.astype(jnp.float32), ((0, 0), (1, 1), (1, 1)))
    mixed = jnp.zeros(preact.shape, jnp.float32)
    for tap_row in range(3):
        for tap_col in range(3):
            window = hidden_pad[:, tap_row:tap_row + n_rows, tap_col:tap_col + n_cols]
            mixed = mixed + jnp.einsum('crw,cd->drw', window, mix32[tap_row, tap_col])
    cot32 = cotangent.astype(jnp.float32)
    cot_pad = jnp.pad(cot32, ((0, 0), (1, 1), (1, 1)))
    mix_terms = []
    grad_hidden = jnp.zeros(preact.shape, jnp.float32)
    for tap_row in range(3):
        for tap_col in range(3):
            window = hidden_pad[:, tap_row:tap_row + n_rows, tap_col:tap_col + n_cols]
            mix_terms.append(jnp.einsum('crw,drw->cd', window, cot32))
            back = cot_pad[:, 2 - tap_row:2 - tap_row + n_rows, 2 - tap_col:2 - tap_col + n_cols]
            grad_hidden = grad_hidden + jnp.einsum('drw,cd->crw', back, mix32[tap_row, tap_col])
    grad_mix = jnp.stack(mix_terms, 1).reshape(mix32.shape[2], 3, 3, mix32.shape[3]) * scale
    slope = normal_cdf(preact) + preact * normal_pdf(preact)
    grad_pre = (grad_hidden * slope).astype(jnp.bfloat16).astype(jnp.float32)
    grad_down = jnp.einsum('crawb,drw->cabd', patches, grad_pre) * scale
    grad_image = jnp.einsum('drw,abcd->crawb', grad_pre, down32).reshape(in_chan, in_rows, in_cols)
    return (mixed.astype(jnp.bfloat16), grad_mix, grad_down, grad_image.astype(jnp.bfloat16))
```

```python
import math

import jax
import jax.numpy as jnp
from jax import lax
from jax.sharding import PartitionSpec as P


def with_halo(block, sides, width):
    for axis, dim in sides:
        count = lax.axis_size(axis)
        forward = [(i, i + 1) for i in range(count - 1)]
        backward = [(target, source) for source, target in forward]
        low = lax.ppermute(
            lax.slice_in_dim(block, block.shape[dim] - width, None, axis=dim), axis, forward
        )
        high = lax.ppermute(lax.slice_in_dim(block, 0, width, axis=dim), axis, backward)
        block = jnp.concatenate([low, block, high], axis=dim)
    return block


def normal_cdf(value):
    return 0.5 * (1.0 + jax.scipy.special.erf(value / math.sqrt(2.0)))


def normal_pdf(value):
    return jnp.exp(-0.5 * value * value) / math.sqrt(2.0 * math.pi)


def per_device(image, w_down, w_mix, cotangent):
    n_tile = lax.axis_size("tile")
    own_out = cotangent.shape[0]
    n_rows = cotangent.shape[1]
    n_cols = cotangent.shape[2]
    own_in = image.shape[0]
    scale = 1.0 / math.sqrt(n_rows * n_tile * n_cols)
    wide_image = lax.all_gather(image, "chan", axis=0, tiled=True)
    in_chan = wide_image.shape[0]
    patches = wide_image.reshape(in_chan, n_rows, 2, n_cols, 2)
    preact = jnp.einsum("crawb,abcd->drw", patches, w_down, preferred_element_type=jnp.float32)
    hidden = (preact * normal_cdf(preact)).astype(jnp.bfloat16)
    plain = lax.all_gather(hidden, "chan", axis=0, tiled=True)
    full_hidden = with_halo(plain, (("tile", 1),), 1)
    hidden_pad = jnp.pad(full_hidden, ((0, 0), (0, 0), (1, 1)))
    all_chan = hidden_pad.shape[0]
    mixed_sum = jnp.zeros((own_out, n_rows, n_cols), jnp.float32)
    for tap_row in range(3):
        for tap_col in range(3):
            window = hidden_pad[:, tap_row : tap_row + n_rows, tap_col : tap_col + n_cols]
            mixed_sum = mixed_sum + jnp.einsum(
                "crw,cd->drw", window, w_mix[tap_row, tap_col], preferred_element_type=jnp.float32
            )
    mixed = mixed_sum.astype(jnp.bfloat16)
    cot_rimmed = with_halo(cotangent, (("tile", 1),), 1)
    part = hidden_pad
    terms = []
    for tap_row in range(3):
        for tap_col in range(3):
            window = part[:, tap_row : tap_row + n_rows, tap_col : tap_col + n_cols]
            terms.append(
                jnp.einsum("crw,drw->cd", window, cotangent, preferred_element_type=jnp.float32)
            )
    grad_mix = (
        lax.psum_scatter(
            jnp.stack(terms, 1).reshape(all_chan // n_tile * lax.axis_size("tile"), 3, 3, own_out),
            "tile",
            scatter_dimension=0,
            tiled=True,
        )
        * scale
    )
    cot_pad = jnp.pad(cot_rimmed, ((0, 0), (0, 0), (1, 1)))
    total = jnp.zeros((own_out * lax.axis_size("chan"), n_rows, n_cols), jnp.float32)
    for tap_row in range(3):
        for tap_col in range(3):
            back = cot_pad[
                :, 2 - tap_row : 2 - tap_row + n_rows, 2 - tap_col : 2 - tap_col + n_cols
            ]
            filters = w_mix[tap_row, tap_col]
            total = total + jnp.einsum(
                "drw,cd->crw", back, filters, preferred_element_type=jnp.float32
            )
    grad_hidden = lax.psum_scatter(total, "chan", scatter_dimension=0, tiled=True)
    slope = normal_cdf(preact) + preact * normal_pdf(preact)
    grad_pre = (grad_hidden * slope).astype(jnp.bfloat16)
    part = patches
    grad_down = (
        lax.psum_scatter(
            jnp.einsum("crawb,drw->cabd", part, grad_pre, preferred_element_type=jnp.float32),
            "tile",
            scatter_dimension=0,
            tiled=True,
        )
        * scale
    )
    down_turned = lax.all_to_all(w_down, "chan", split_axis=2, concat_axis=3, tiled=True)
    filters = down_turned
    term = jnp.einsum(
        "drw,abcd->crawb",
        lax.all_gather(grad_pre, "chan", axis=0, tiled=True),
        filters,
        preferred_element_type=jnp.float32,
    )
    grad_image = term.reshape(jnp.zeros((own_in, 2 * n_rows, 2 * n_cols), jnp.float32).shape)
    return (mixed, grad_mix, grad_down, grad_image.astype(jnp.bfloat16))


def flip(block, axis, mask):
    count = lax.axis_size(axis)
    return lax.ppermute(block, axis, [(i, i ^ mask) for i in range(count)])


def tap_sum(padded, weights, n_rows, n_cols, back):
    total = None
    for i in range(3):
        for j in range(3):
            r, c = (2 - i, 2 - j) if back else (i, j)
            window = padded[:, r : r + n_rows, c : c + n_cols]
            form = "drw,cd->crw" if back else "crw,cd->drw"
            term = jnp.einsum(form, window, weights[i, j], preferred_element_type=jnp.float32)
            total = term if total is None else total + term
    return total


def halve(block, dim, bit):
    mine = (lax.axis_index("tile") >> bit) & 1
    keep = lax.dynamic_index_in_dim(block, mine, dim, keepdims=False)
    send = lax.dynamic_index_in_dim(block, 1 - mine, dim, keepdims=False)
    got = flip(send.astype(jnp.bfloat16), "tile", 1 << bit)
    return keep.astype(jnp.float32) + got.astype(jnp.float32)


def reduce_halves(own, other, top):
    taps, half, depth = own.shape
    share = half >> top
    own_bits = list(range(top))
    other_bits = own_bits[:1] + own_bits[:0:-1]
    sums = []
    for block, order in ((own, own_bits), (other, other_bits)):
        left = list(range(top))[::-1]
        block = block.reshape((taps,) + (2,) * top + (share, depth))
        for bit in order:
            block = halve(block, 1 + left.index(bit), bit)
            left.remove(bit)
        sums.append(block)
    here = (lax.axis_index("tile") >> top) == lax.axis_index("chan")
    keep = jnp.where(here, sums[0], sums[1])
    send = jnp.where(here, sums[1], sums[0])
    return keep + flip(send.astype(jnp.bfloat16), "tile", 1 << top).astype(jnp.float32)


def edge_rows(block, cross):
    n_tile = lax.axis_size("tile")
    down, up = [], []
    for k in range(2):
        to = (1 - k if cross else k) * n_tile
        for i in range(n_tile - 1):
            down.append((k * n_tile + i, to + i + 1))
            up.append((k * n_tile + i + 1, to + i))
    low = lax.ppermute(block[:, -1:], ("chan", "tile"), down)
    high = lax.ppermute(block[:, :1], ("chan", "tile"), up)
    return low, high


def rimmed(block, edges):
    low, high = edges
    return jnp.pad(jnp.concatenate([low, block, high], axis=1), ((0, 0), (0, 0), (1, 1)))


def pair_device(image, w_down, w_mix, cotangent):
    bf16, f32 = jnp.bfloat16, jnp.float32
    n_tile = lax.axis_size("tile")
    top = n_tile.bit_length() - 2
    own_out, n_rows, n_cols = cotangent.shape
    own_in = image.shape[0]
    scale = 1.0 / math.sqrt(n_rows * n_tile * n_cols)
    k = lax.axis_index("chan")

    def part(weights, which, dim, size):
        return lax.dynamic_slice_in_dim(weights, which * size, size, dim)

    image_far = flip(image, "chan", 1)
    cot_edges = edge_rows(cotangent, False)
    down_own, down_far = part(w_down, k, 2, own_in), part(w_down, 1 - k, 2, own_in)
    mix_own, mix_far = part(w_mix, k, 2, own_out), part(w_mix, 1 - k, 2, own_out)
    down_back = flip(down_far, "chan", 1)

    cot_pad = rimmed(cotangent, cot_edges)
    away = tap_sum(cot_pad, mix_far, n_rows, n_cols, True)
    got = flip(away.astype(bf16), "chan", 1)
    grad_hidden = tap_sum(cot_pad, mix_own, n_rows, n_cols, True)

    def taps_of(block):
        return block.reshape(own_in, n_rows, 2, n_cols, 2)

    near, far = taps_of(image), taps_of(image_far)
    preact = jnp.einsum("crawb,abcd->drw", near, down_own, preferred_element_type=f32)
    preact = preact + jnp.einsum("crawb,abcd->drw", far, down_far, preferred_element_type=f32)
    cdf = normal_cdf(preact)
    hidden = (preact * cdf).astype(bf16)
    hidden_far = flip(hidden, "chan", 1)
    own_edges, far_edges = edge_rows(hidden, False), edge_rows(hidden, True)

    slope = cdf + preact * normal_pdf(preact)
    grad_pre = ((grad_hidden + got.astype(f32)) * slope).astype(bf16)
    grad_pre_far = flip(grad_pre, "chan", 1)

    def mix_terms(padded):
        terms = []
        for i in range(3):
            for j in range(3):
                window = padded[:, i : i + n_rows, j : j + n_cols]
                terms.append(
                    jnp.einsum("crw,drw->cd", window, cotangent, preferred_element_type=f32)
                )
        return jnp.stack(terms)

    own_pad = rimmed(hidden, own_edges)
    far_pad = rimmed(hidden_far, far_edges)
    grad_mix = reduce_halves(mix_terms(own_pad), mix_terms(far_pad), top) * scale
    grad_mix = grad_mix.transpose(1, 0, 2).reshape(-1, 3, 3, own_out)
    mixed = tap_sum(own_pad, mix_own, n_rows, n_cols, False)
    mixed = (mixed + tap_sum(far_pad, mix_far, n_rows, n_cols, False)).astype(bf16)

    def down_terms(patches):
        term = jnp.einsum("crawb,drw->abcd", patches, grad_pre, preferred_element_type=f32)
        return term.reshape(4, own_in, own_out)

    grad_down = reduce_halves(down_terms(near), down_terms(far), top) * scale
    grad_down = grad_down.transpose(1, 0, 2).reshape(-1, 2, 2, own_out)
    term = jnp.einsum("drw,abcd->crawb", grad_pre, down_own, preferred_element_type=f32)
    term = term + jnp.einsum(
        "drw,abcd->crawb", grad_pre_far, down_back, preferred_element_type=f32
    )
    return (mixed, grad_mix, grad_down, term.astype(bf16).reshape(image.shape))


def solution(mesh):
    sizes = dict(mesh.shape)
    n_tile = sizes["tile"]
    paired = sizes["chan"] == 2 and n_tile > 1 and n_tile & (n_tile - 1) == 0
    return jax.shard_map(
        pair_device if paired else per_device,
        mesh=mesh,
        in_specs=(
            P("chan", "tile", None),
            P(None, None, None, "chan"),
            P(None, None, None, "chan"),
            P("chan", "tile", None),
        ),
        out_specs=(
            P("chan", "tile", None),
            P("tile", None, None, "chan"),
            P("tile", None, None, "chan"),
            P("chan", "tile", None),
        ),
        check_vma=False,
    )
```

```python
import math

import jax
import jax.numpy as jnp
from jax import lax
from jax.sharding import PartitionSpec as P


def with_halo(block, sides, width):
    for axis, dim in sides:
        count = lax.axis_size(axis)
        forward = [(i, i + 1) for i in range(count - 1)]
        backward = [(target, source) for source, target in forward]
        low = lax.ppermute(
            lax.slice_in_dim(block, block.shape[dim] - width, None, axis=dim), axis, forward
        )
        high = lax.ppermute(lax.slice_in_dim(block, 0, width, axis=dim), axis, backward)
        block = jnp.concatenate([low, block, high], axis=dim)
    return block


def normal_cdf(value):
    return 0.5 * (1.0 + jax.scipy.special.erf(value / math.sqrt(2.0)))


def normal_pdf(value):
    return jnp.exp(-0.5 * value * value) / math.sqrt(2.0 * math.pi)


def per_device(image, w_down, w_mix, cotangent):
    n_tile = lax.axis_size("tile")
    own_out = cotangent.shape[0]
    n_rows = cotangent.shape[1]
    n_cols = cotangent.shape[2]
    own_in = image.shape[0]
    scale = 1.0 / math.sqrt(n_rows * n_tile * n_cols)
    wide_image = lax.all_gather(image, "chan", axis=0, tiled=True)
    in_chan = wide_image.shape[0]
    patches = wide_image.reshape(in_chan, n_rows, 2, n_cols, 2)
    preact = jnp.einsum("crawb,abcd->drw", patches, w_down, preferred_element_type=jnp.float32)
    hidden = (preact * normal_cdf(preact)).astype(jnp.bfloat16)
    plain = lax.all_gather(hidden, "chan", axis=0, tiled=True)
    full_hidden = with_halo(plain, (("tile", 1),), 1)
    hidden_pad = jnp.pad(full_hidden, ((0, 0), (0, 0), (1, 1)))
    all_chan = hidden_pad.shape[0]
    mixed_sum = jnp.zeros((own_out, n_rows, n_cols), jnp.float32)
    for tap_row in range(3):
        for tap_col in range(3):
            window = hidden_pad[:, tap_row : tap_row + n_rows, tap_col : tap_col + n_cols]
            mixed_sum = mixed_sum + jnp.einsum(
                "crw,cd->drw", window, w_mix[tap_row, tap_col], preferred_element_type=jnp.float32
            )
    mixed = mixed_sum.astype(jnp.bfloat16)
    cot_rimmed = with_halo(cotangent, (("tile", 1),), 1)
    part = hidden_pad
    terms = []
    for tap_row in range(3):
        for tap_col in range(3):
            window = part[:, tap_row : tap_row + n_rows, tap_col : tap_col + n_cols]
            terms.append(
                jnp.einsum("crw,drw->cd", window, cotangent, preferred_element_type=jnp.float32)
            )
    grad_mix = (
        lax.psum_scatter(
            jnp.stack(terms, 1).reshape(all_chan // n_tile * lax.axis_size("tile"), 3, 3, own_out),
            "tile",
            scatter_dimension=0,
            tiled=True,
        )
        * scale
    )
    cot_pad = jnp.pad(cot_rimmed, ((0, 0), (0, 0), (1, 1)))
    total = jnp.zeros((own_out * lax.axis_size("chan"), n_rows, n_cols), jnp.float32)
    for tap_row in range(3):
        for tap_col in range(3):
            back = cot_pad[
                :, 2 - tap_row : 2 - tap_row + n_rows, 2 - tap_col : 2 - tap_col + n_cols
            ]
            filters = w_mix[tap_row, tap_col]
            total = total + jnp.einsum(
                "drw,cd->crw", back, filters, preferred_element_type=jnp.float32
            )
    grad_hidden = lax.psum_scatter(total, "chan", scatter_dimension=0, tiled=True)
    slope = normal_cdf(preact) + preact * normal_pdf(preact)
    grad_pre = (grad_hidden * slope).astype(jnp.bfloat16)
    part = patches
    grad_down = (
        lax.psum_scatter(
            jnp.einsum("crawb,drw->cabd", part, grad_pre, preferred_element_type=jnp.float32),
            "tile",
            scatter_dimension=0,
            tiled=True,
        )
        * scale
    )
    down_turned = lax.all_to_all(w_down, "chan", split_axis=2, concat_axis=3, tiled=True)
    filters = down_turned
    term = jnp.einsum(
        "drw,abcd->crawb",
        lax.all_gather(grad_pre, "chan", axis=0, tiled=True),
        filters,
        preferred_element_type=jnp.float32,
    )
    grad_image = term.reshape(jnp.zeros((own_in, 2 * n_rows, 2 * n_cols), jnp.float32).shape)
    return (mixed, grad_mix, grad_down, grad_image.astype(jnp.bfloat16))


def flip(block, axis, mask):
    count = lax.axis_size(axis)
    return lax.ppermute(block, axis, [(i, i ^ mask) for i in range(count)])


def tap_sum(padded, weights, n_rows, n_cols, back):
    total = None
    for i in range(3):
        for j in range(3):
            r, c = (2 - i, 2 - j) if back else (i, j)
            window = padded[:, r : r + n_rows, c : c + n_cols]
            form = "drw,cd->crw" if back else "crw,cd->drw"
            term = jnp.einsum(form, window, weights[i, j], preferred_element_type=jnp.float32)
            total = term if total is None else total + term
    return total


def halve(block, dim, bit):
    mine = (lax.axis_index("tile") >> bit) & 1
    keep = lax.dynamic_index_in_dim(block, mine, dim, keepdims=False)
    send = lax.dynamic_index_in_dim(block, 1 - mine, dim, keepdims=False)
    got = flip(send.astype(jnp.bfloat16), "tile", 1 << bit)
    return keep.astype(jnp.float32) + got.astype(jnp.float32)


def reduce_halves(own, other, top, swapped=None):
    taps, half, depth = own.shape
    share = half >> top
    own_bits = list(range(top))
    other_bits = own_bits[:1] + own_bits[:0:-1]
    sums = []
    for block, order in ((own, own_bits), (other, other_bits)):
        left = list(range(top))[::-1]
        block = block.reshape((taps,) + (2,) * top + (share, depth))
        for bit in order:
            block = halve(block, 1 + left.index(bit), bit)
            left.remove(bit)
        sums.append(block)
    if swapped is not None:
        sums, swapped = lax.optimization_barrier((sums, swapped))
    here = (lax.axis_index("tile") >> top) == lax.axis_index("chan")
    keep = jnp.where(here, sums[0], sums[1])
    send = jnp.where(here, sums[1], sums[0])
    total = keep + flip(send.astype(jnp.bfloat16), "tile", 1 << top).astype(jnp.float32)
    return total if swapped is None else (total, swapped)


def edge_rows(block, cross):
    n_tile = lax.axis_size("tile")
    down, up = [], []
    for k in range(2):
        to = (1 - k if cross else k) * n_tile
        for i in range(n_tile - 1):
            down.append((k * n_tile + i, to + i + 1))
            up.append((k * n_tile + i + 1, to + i))
    low = lax.ppermute(block[:, -1:], ("chan", "tile"), down)
    high = lax.ppermute(block[:, :1], ("chan", "tile"), up)
    return low, high


def rimmed(block, edges):
    low, high = edges
    return jnp.pad(jnp.concatenate([low, block, high], axis=1), ((0, 0), (0, 0), (1, 1)))


def pair_device(image, w_down, w_mix, cotangent):
    bf16, f32 = jnp.bfloat16, jnp.float32
    n_tile = lax.axis_size("tile")
    top = n_tile.bit_length() - 2
    own_out, n_rows, n_cols = cotangent.shape
    own_in = image.shape[0]
    scale = 1.0 / math.sqrt(n_rows * n_tile * n_cols)
    k = lax.axis_index("chan")

    def part(weights, which, dim, size):
        return lax.dynamic_slice_in_dim(weights, which * size, size, dim)

    deep, cotangent = lax.optimization_barrier((image.transpose(1, 2, 0), cotangent))
    deep_far = flip(deep, "chan", 1)
    cot_edges = edge_rows(cotangent, False)
    down_own, down_far = part(w_down, k, 2, own_in), part(w_down, 1 - k, 2, own_in)
    mix_own, mix_far = part(w_mix, k, 2, own_out), part(w_mix, 1 - k, 2, own_out)

    cot_pad = rimmed(cotangent, cot_edges)
    away = tap_sum(cot_pad, mix_far, n_rows, n_cols, True).astype(bf16)
    grad_hidden = tap_sum(cot_pad, mix_own, n_rows, n_cols, True)

    def taps_of(block):
        return block.reshape(n_rows, 2, n_cols, 2, own_in)

    near, far = taps_of(deep), taps_of(deep_far)
    preact = jnp.einsum("rawbc,abcd->drw", near, down_own, preferred_element_type=f32)
    preact = preact + jnp.einsum("rawbc,abcd->drw", far, down_far, preferred_element_type=f32)
    cdf = normal_cdf(preact)
    hidden = (preact * cdf).astype(bf16)
    hidden_far = flip(hidden, "chan", 1)
    own_edges, far_edges = edge_rows(hidden, False), edge_rows(hidden, True)
    hidden_far, away, down_far = lax.optimization_barrier((hidden_far, away, down_far))
    got = flip(away, "chan", 1)
    down_back = flip(down_far, "chan", 1)

    slope = cdf + preact * normal_pdf(preact)
    grad_pre = ((grad_hidden + got.astype(f32)) * slope).astype(bf16)
    grad_pre_far = flip(grad_pre, "chan", 1)

    def mix_terms(padded):
        terms = []
        for i in range(3):
            for j in range(3):
                window = padded[:, i : i + n_rows, j : j + n_cols]
                terms.append(
                    jnp.einsum("crw,drw->cd", window, cotangent, preferred_element_type=f32)
                )
        return jnp.stack(terms)

    own_pad = rimmed(hidden, own_edges)
    far_pad = rimmed(hidden_far, far_edges)
    grad_mix = reduce_halves(mix_terms(own_pad), mix_terms(far_pad), top) * scale
    grad_mix = grad_mix.transpose(1, 0, 2).reshape(-1, 3, 3, own_out)
    mixed = tap_sum(own_pad, mix_own, n_rows, n_cols, False)
    mixed = (mixed + tap_sum(far_pad, mix_far, n_rows, n_cols, False)).astype(bf16)

    def down_terms(patches):
        term = jnp.einsum("rawbc,drw->abcd", patches, grad_pre, preferred_element_type=f32)
        return term.reshape(4, own_in, own_out)

    grad_down, grad_pre_far = reduce_halves(
        down_terms(near), down_terms(far), top, grad_pre_far
    )
    grad_down = (grad_down * scale).transpose(1, 0, 2).reshape(-1, 2, 2, own_out)
    term = jnp.einsum("drw,abcd->crawb", grad_pre, down_own, preferred_element_type=f32)
    term = term + jnp.einsum(
        "drw,abcd->crawb", grad_pre_far, down_back, preferred_element_type=f32
    )
    return (mixed, grad_mix, grad_down, term.astype(bf16).reshape(image.shape))


def solution(mesh):
    sizes = dict(mesh.shape)
    n_tile = sizes["tile"]
    paired = sizes["chan"] == 2 and n_tile > 1 and n_tile & (n_tile - 1) == 0
    return jax.shard_map(
        pair_device if paired else per_device,
        mesh=mesh,
        in_specs=(
            P("chan", "tile", None),
            P(None, None, None, "chan"),
            P(None, None, None, "chan"),
            P("chan", "tile", None),
        ),
        out_specs=(
            P("chan", "tile", None),
            P("tile", None, None, "chan"),
            P("tile", None, None, "chan"),
            P("chan", "tile", None),
        ),
        check_vma=False,
    )
```

```python
import math

import jax
import jax.numpy as jnp
from jax import lax
from jax.sharding import PartitionSpec as P


def with_halo(block, sides, width):
    for axis, dim in sides:
        count = lax.axis_size(axis)
        forward = [(i, i + 1) for i in range(count - 1)]
        backward = [(target, source) for source, target in forward]
        low = lax.ppermute(
            lax.slice_in_dim(block, block.shape[dim] - width, None, axis=dim), axis, forward
        )
        high = lax.ppermute(lax.slice_in_dim(block, 0, width, axis=dim), axis, backward)
        block = jnp.concatenate([low, block, high], axis=dim)
    return block


def normal_cdf(value):
    return 0.5 * (1.0 + jax.scipy.special.erf(value / math.sqrt(2.0)))


def normal_pdf(value):
    return jnp.exp(-0.5 * value * value) / math.sqrt(2.0 * math.pi)


def per_device(image, w_down, w_mix, cotangent):
    n_tile = lax.axis_size("tile")
    own_out = cotangent.shape[0]
    n_rows = cotangent.shape[1]
    n_cols = cotangent.shape[2]
    own_in = image.shape[0]
    scale = 1.0 / math.sqrt(n_rows * n_tile * n_cols)
    wide_image = lax.all_gather(image, "chan", axis=0, tiled=True)
    in_chan = wide_image.shape[0]
    patches = wide_image.reshape(in_chan, n_rows, 2, n_cols, 2)
    preact = jnp.einsum("crawb,abcd->drw", patches, w_down, preferred_element_type=jnp.float32)
    hidden = (preact * normal_cdf(preact)).astype(jnp.bfloat16)
    plain = lax.all_gather(hidden, "chan", axis=0, tiled=True)
    full_hidden = with_halo(plain, (("tile", 1),), 1)
    hidden_pad = jnp.pad(full_hidden, ((0, 0), (0, 0), (1, 1)))
    all_chan = hidden_pad.shape[0]
    mixed_sum = jnp.zeros((own_out, n_rows, n_cols), jnp.float32)
    for tap_row in range(3):
        for tap_col in range(3):
            window = hidden_pad[:, tap_row : tap_row + n_rows, tap_col : tap_col + n_cols]
            mixed_sum = mixed_sum + jnp.einsum(
                "crw,cd->drw", window, w_mix[tap_row, tap_col], preferred_element_type=jnp.float32
            )
    mixed = mixed_sum.astype(jnp.bfloat16)
    cot_rimmed = with_halo(cotangent, (("tile", 1),), 1)
    part = hidden_pad
    terms = []
    for tap_row in range(3):
        for tap_col in range(3):
            window = part[:, tap_row : tap_row + n_rows, tap_col : tap_col + n_cols]
            terms.append(
                jnp.einsum("crw,drw->cd", window, cotangent, preferred_element_type=jnp.float32)
            )
    grad_mix = (
        lax.psum_scatter(
            jnp.stack(terms, 1).reshape(all_chan // n_tile * lax.axis_size("tile"), 3, 3, own_out),
            "tile",
            scatter_dimension=0,
            tiled=True,
        )
        * scale
    )
    cot_pad = jnp.pad(cot_rimmed, ((0, 0), (0, 0), (1, 1)))
    total = jnp.zeros((own_out * lax.axis_size("chan"), n_rows, n_cols), jnp.float32)
    for tap_row in range(3):
        for tap_col in range(3):
            back = cot_pad[
                :, 2 - tap_row : 2 - tap_row + n_rows, 2 - tap_col : 2 - tap_col + n_cols
            ]
            filters = w_mix[tap_row, tap_col]
            total = total + jnp.einsum(
                "drw,cd->crw", back, filters, preferred_element_type=jnp.float32
            )
    grad_hidden = lax.psum_scatter(total, "chan", scatter_dimension=0, tiled=True)
    slope = normal_cdf(preact) + preact * normal_pdf(preact)
    grad_pre = (grad_hidden * slope).astype(jnp.bfloat16)
    part = patches
    grad_down = (
        lax.psum_scatter(
            jnp.einsum("crawb,drw->cabd", part, grad_pre, preferred_element_type=jnp.float32),
            "tile",
            scatter_dimension=0,
            tiled=True,
        )
        * scale
    )
    down_turned = lax.all_to_all(w_down, "chan", split_axis=2, concat_axis=3, tiled=True)
    filters = down_turned
    term = jnp.einsum(
        "drw,abcd->crawb",
        lax.all_gather(grad_pre, "chan", axis=0, tiled=True),
        filters,
        preferred_element_type=jnp.float32,
    )
    grad_image = term.reshape(jnp.zeros((own_in, 2 * n_rows, 2 * n_cols), jnp.float32).shape)
    return (mixed, grad_mix, grad_down, grad_image.astype(jnp.bfloat16))


def flip(block, axis, mask):
    count = lax.axis_size(axis)
    return lax.ppermute(block, axis, [(i, i ^ mask) for i in range(count)])


def tap_sum(padded, weights, n_rows, n_cols, back):
    total = None
    for i in range(3):
        for j in range(3):
            r, c = (2 - i, 2 - j) if back else (i, j)
            window = padded[:, r : r + n_rows, c : c + n_cols]
            form = "drw,cd->crw" if back else "crw,cd->drw"
            term = jnp.einsum(form, window, weights[i, j], preferred_element_type=jnp.float32)
            total = term if total is None else total + term
    return total


def halve(block, dim, bit):
    mine = (lax.axis_index("tile") >> bit) & 1
    keep = lax.dynamic_index_in_dim(block, mine, dim, keepdims=False)
    send = lax.dynamic_index_in_dim(block, 1 - mine, dim, keepdims=False)
    got = flip(send.astype(jnp.bfloat16), "tile", 1 << bit)
    return keep.astype(jnp.float32) + got.astype(jnp.float32)


def reduce_halves(own, other, top, swapped=None):
    taps, half, depth = own.shape
    share = half >> top
    own_bits = list(range(top))
    other_bits = own_bits[:1] + own_bits[:0:-1]
    sums = []
    for block, order in ((own, own_bits), (other, other_bits)):
        left = list(range(top))[::-1]
        block = block.reshape((taps,) + (2,) * top + (share, depth))
        for bit in order:
            block = halve(block, 1 + left.index(bit), bit)
            left.remove(bit)
        sums.append(block)
    if swapped is not None:
        sums, swapped = lax.optimization_barrier((sums, swapped))
    here = (lax.axis_index("tile") >> top) == lax.axis_index("chan")
    keep = jnp.where(here, sums[0], sums[1])
    send = jnp.where(here, sums[1], sums[0])
    total = keep + flip(send.astype(jnp.bfloat16), "tile", 1 << top).astype(jnp.float32)
    return total if swapped is None else (total, swapped)


def edge_rows(block, cross):
    n_tile = lax.axis_size("tile")
    down, up = [], []
    for k in range(2):
        to = (1 - k if cross else k) * n_tile
        for i in range(n_tile - 1):
            down.append((k * n_tile + i, to + i + 1))
            up.append((k * n_tile + i + 1, to + i))
    low = lax.ppermute(block[:, -1:], ("chan", "tile"), down)
    high = lax.ppermute(block[:, :1], ("chan", "tile"), up)
    return low, high


def rimmed(block, edges):
    low, high = edges
    return jnp.pad(jnp.concatenate([low, block, high], axis=1), ((0, 0), (0, 0), (1, 1)))


def pair_device(image, w_down, w_mix, cotangent):
    bf16, f32 = jnp.bfloat16, jnp.float32
    n_tile = lax.axis_size("tile")
    top = n_tile.bit_length() - 2
    own_out, n_rows, n_cols = cotangent.shape
    own_in = image.shape[0]
    scale = 1.0 / math.sqrt(n_rows * n_tile * n_cols)
    k = lax.axis_index("chan")

    def part(weights, which, dim, size):
        return lax.dynamic_slice_in_dim(weights, which * size, size, dim)

    deep, cotangent = lax.optimization_barrier((image.transpose(1, 2, 0), cotangent))
    deep_far = flip(deep, "chan", 1)
    cot_edges = edge_rows(cotangent, False)
    down_own, down_far = part(w_down, k, 2, own_in), part(w_down, 1 - k, 2, own_in)
    mix_own, mix_far = part(w_mix, k, 2, own_out), part(w_mix, 1 - k, 2, own_out)

    cot_pad = rimmed(cotangent, cot_edges)
    away = tap_sum(cot_pad, mix_far, n_rows, n_cols, True).astype(bf16)
    grad_hidden = tap_sum(cot_pad, mix_own, n_rows, n_cols, True)

    def taps_of(block):
        return block.reshape(n_rows, 2, n_cols, 2, own_in)

    near, far = taps_of(deep), taps_of(deep_far)
    preact = jnp.einsum("rawbc,abcd->drw", near, down_own, preferred_element_type=f32)
    preact = preact + jnp.einsum("rawbc,abcd->drw", far, down_far, preferred_element_type=f32)
    cdf = normal_cdf(preact)
    hidden = (preact * cdf).astype(bf16)
    hidden, away = lax.optimization_barrier((hidden, away))
    hidden_far = flip(hidden, "chan", 1)
    own_edges, far_edges = edge_rows(hidden, False), edge_rows(hidden, True)
    hidden_far, down_far = lax.optimization_barrier((hidden_far, down_far))
    got = flip(away, "chan", 1)
    down_back = flip(down_far, "chan", 1)

    slope = cdf + preact * normal_pdf(preact)
    grad_pre = ((grad_hidden + got.astype(f32)) * slope).astype(bf16)
    grad_pre_far = flip(grad_pre, "chan", 1)

    def mix_terms(padded):
        terms = []
        for i in range(3):
            for j in range(3):
                window = padded[:, i : i + n_rows, j : j + n_cols]
                terms.append(
                    jnp.einsum("crw,drw->cd", window, cotangent, preferred_element_type=f32)
                )
        return jnp.stack(terms)

    own_pad = rimmed(hidden, own_edges)
    far_pad = rimmed(hidden_far, far_edges)
    grad_mix = reduce_halves(mix_terms(own_pad), mix_terms(far_pad), top) * scale
    grad_mix = grad_mix.transpose(1, 0, 2).reshape(-1, 3, 3, own_out)
    mixed = tap_sum(own_pad, mix_own, n_rows, n_cols, False)
    mixed = (mixed + tap_sum(far_pad, mix_far, n_rows, n_cols, False)).astype(bf16)

    def down_terms(patches):
        term = jnp.einsum("rawbc,drw->abcd", patches, grad_pre, preferred_element_type=f32)
        return term.reshape(4, own_in, own_out)

    grad_down, grad_pre_far = reduce_halves(
        down_terms(near), down_terms(far), top, grad_pre_far
    )
    grad_down = (grad_down * scale).transpose(1, 0, 2).reshape(-1, 2, 2, own_out)
    term = jnp.einsum("drw,abcd->crawb", grad_pre, down_own, preferred_element_type=f32)
    term = term + jnp.einsum(
        "drw,abcd->crawb", grad_pre_far, down_back, preferred_element_type=f32
    )
    return (mixed, grad_mix, grad_down, term.astype(bf16).reshape(image.shape))


def solution(mesh):
    sizes = dict(mesh.shape)
    n_tile = sizes["tile"]
    paired = sizes["chan"] == 2 and n_tile > 1 and n_tile & (n_tile - 1) == 0
    return jax.shard_map(
        pair_device if paired else per_device,
        mesh=mesh,
        in_specs=(
            P("chan", "tile", None),
            P(None, None, None, "chan"),
            P(None, None, None, "chan"),
            P("chan", "tile", None),
        ),
        out_specs=(
            P("chan", "tile", None),
            P("tile", None, None, "chan"),
            P("tile", None, None, "chan"),
            P("chan", "tile", None),
        ),
        check_vma=False,
    )
```

```python
import math

import jax
import jax.numpy as jnp
from jax import lax
from jax.sharding import PartitionSpec as P


def with_halo(block, sides, width):
    for axis, dim in sides:
        count = lax.axis_size(axis)
        forward = [(i, i + 1) for i in range(count - 1)]
        backward = [(target, source) for source, target in forward]
        low = lax.ppermute(
            lax.slice_in_dim(block, block.shape[dim] - width, None, axis=dim), axis, forward
        )
        high = lax.ppermute(lax.slice_in_dim(block, 0, width, axis=dim), axis, backward)
        block = jnp.concatenate([low, block, high], axis=dim)
    return block


def normal_cdf(value):
    return 0.5 * (1.0 + jax.scipy.special.erf(value / math.sqrt(2.0)))


def normal_pdf(value):
    return jnp.exp(-0.5 * value * value) / math.sqrt(2.0 * math.pi)


def per_device(image, w_down, w_mix, cotangent):
    n_tile = lax.axis_size("tile")
    own_out = cotangent.shape[0]
    n_rows = cotangent.shape[1]
    n_cols = cotangent.shape[2]
    own_in = image.shape[0]
    scale = 1.0 / math.sqrt(n_rows * n_tile * n_cols)
    wide_image = lax.all_gather(image, "chan", axis=0, tiled=True)
    in_chan = wide_image.shape[0]
    patches = wide_image.reshape(in_chan, n_rows, 2, n_cols, 2)
    preact = jnp.einsum("crawb,abcd->drw", patches, w_down, preferred_element_type=jnp.float32)
    hidden = (preact * normal_cdf(preact)).astype(jnp.bfloat16)
    plain = lax.all_gather(hidden, "chan", axis=0, tiled=True)
    full_hidden = with_halo(plain, (("tile", 1),), 1)
    hidden_pad = jnp.pad(full_hidden, ((0, 0), (0, 0), (1, 1)))
    all_chan = hidden_pad.shape[0]
    mixed_sum = jnp.zeros((own_out, n_rows, n_cols), jnp.float32)
    for tap_row in range(3):
        for tap_col in range(3):
            window = hidden_pad[:, tap_row : tap_row + n_rows, tap_col : tap_col + n_cols]
            mixed_sum = mixed_sum + jnp.einsum(
                "crw,cd->drw", window, w_mix[tap_row, tap_col], preferred_element_type=jnp.float32
            )
    mixed = mixed_sum.astype(jnp.bfloat16)
    cot_rimmed = with_halo(cotangent, (("tile", 1),), 1)
    part = hidden_pad
    terms = []
    for tap_row in range(3):
        for tap_col in range(3):
            window = part[:, tap_row : tap_row + n_rows, tap_col : tap_col + n_cols]
            terms.append(
                jnp.einsum("crw,drw->cd", window, cotangent, preferred_element_type=jnp.float32)
            )
    grad_mix = (
        lax.psum_scatter(
            jnp.stack(terms, 1).reshape(all_chan // n_tile * lax.axis_size("tile"), 3, 3, own_out),
            "tile",
            scatter_dimension=0,
            tiled=True,
        )
        * scale
    )
    cot_pad = jnp.pad(cot_rimmed, ((0, 0), (0, 0), (1, 1)))
    total = jnp.zeros((own_out * lax.axis_size("chan"), n_rows, n_cols), jnp.float32)
    for tap_row in range(3):
        for tap_col in range(3):
            back = cot_pad[
                :, 2 - tap_row : 2 - tap_row + n_rows, 2 - tap_col : 2 - tap_col + n_cols
            ]
            filters = w_mix[tap_row, tap_col]
            total = total + jnp.einsum(
                "drw,cd->crw", back, filters, preferred_element_type=jnp.float32
            )
    grad_hidden = lax.psum_scatter(total, "chan", scatter_dimension=0, tiled=True)
    slope = normal_cdf(preact) + preact * normal_pdf(preact)
    grad_pre = (grad_hidden * slope).astype(jnp.bfloat16)
    part = patches
    grad_down = (
        lax.psum_scatter(
            jnp.einsum("crawb,drw->cabd", part, grad_pre, preferred_element_type=jnp.float32),
            "tile",
            scatter_dimension=0,
            tiled=True,
        )
        * scale
    )
    down_turned = lax.all_to_all(w_down, "chan", split_axis=2, concat_axis=3, tiled=True)
    filters = down_turned
    term = jnp.einsum(
        "drw,abcd->crawb",
        lax.all_gather(grad_pre, "chan", axis=0, tiled=True),
        filters,
        preferred_element_type=jnp.float32,
    )
    grad_image = term.reshape(jnp.zeros((own_in, 2 * n_rows, 2 * n_cols), jnp.float32).shape)
    return (mixed, grad_mix, grad_down, grad_image.astype(jnp.bfloat16))


def flip(block, axis, mask):
    count = lax.axis_size(axis)
    return lax.ppermute(block, axis, [(i, i ^ mask) for i in range(count)])


def tap_sum(padded, weights, n_rows, n_cols, back):
    total = None
    for i in range(3):
        for j in range(3):
            r, c = (2 - i, 2 - j) if back else (i, j)
            window = padded[:, r : r + n_rows, c : c + n_cols]
            form = "drw,cd->crw" if back else "crw,cd->drw"
            term = jnp.einsum(form, window, weights[i, j], preferred_element_type=jnp.float32)
            total = term if total is None else total + term
    return total


def halve(block, dim, bit):
    mine = (lax.axis_index("tile") >> bit) & 1
    keep = lax.dynamic_index_in_dim(block, mine, dim, keepdims=False)
    send = lax.dynamic_index_in_dim(block, 1 - mine, dim, keepdims=False)
    got = flip(send.astype(jnp.bfloat16), "tile", 1 << bit)
    return keep.astype(jnp.float32) + got.astype(jnp.float32)


def reduce_halves(own, other, top, swapped=None):
    taps, half, depth = own.shape
    share = half >> top
    own_bits = list(range(top))
    other_bits = own_bits[:1] + own_bits[:0:-1]
    sums = []
    parts = ((own, own_bits), (other, other_bits))
    if swapped is not None:
        parts = ((jnp.concatenate([own, other]), own_bits),)
    for block, order in parts:
        left = list(range(top))[::-1]
        block = block.reshape((block.shape[0],) + (2,) * top + (share, depth))
        for bit in order:
            block = halve(block, 1 + left.index(bit), bit)
            left.remove(bit)
        sums.append(block)
    if swapped is not None:
        sums = [sums[0][:taps], sums[0][taps:]]
        sums, swapped = lax.optimization_barrier((sums, swapped))
    here = (lax.axis_index("tile") >> top) == lax.axis_index("chan")
    keep = jnp.where(here, sums[0], sums[1])
    send = jnp.where(here, sums[1], sums[0])
    total = keep + flip(send.astype(jnp.bfloat16), "tile", 1 << top).astype(jnp.float32)
    return total if swapped is None else (total, swapped)


def edge_rows(block, cross):
    n_tile = lax.axis_size("tile")
    down, up = [], []
    for k in range(2):
        to = (1 - k if cross else k) * n_tile
        for i in range(n_tile - 1):
            down.append((k * n_tile + i, to + i + 1))
            up.append((k * n_tile + i + 1, to + i))
    low = lax.ppermute(block[:, -1:], ("chan", "tile"), down)
    high = lax.ppermute(block[:, :1], ("chan", "tile"), up)
    return low, high


def rimmed(block, edges):
    low, high = edges
    return jnp.pad(jnp.concatenate([low, block, high], axis=1), ((0, 0), (0, 0), (1, 1)))


def pair_device(image, w_down, w_mix, cotangent):
    bf16, f32 = jnp.bfloat16, jnp.float32
    n_tile = lax.axis_size("tile")
    top = n_tile.bit_length() - 2
    own_out, n_rows, n_cols = cotangent.shape
    own_in = image.shape[0]
    scale = 1.0 / math.sqrt(n_rows * n_tile * n_cols)
    k = lax.axis_index("chan")

    def part(weights, which, dim, size):
        return lax.dynamic_slice_in_dim(weights, which * size, size, dim)

    deep, cotangent = lax.optimization_barrier((image.transpose(1, 2, 0), cotangent))
    deep_far = flip(deep, "chan", 1)
    cot_edges = edge_rows(cotangent, False)
    down_own, down_far = part(w_down, k, 2, own_in), part(w_down, 1 - k, 2, own_in)
    mix_own, mix_far = part(w_mix, k, 2, own_out), part(w_mix, 1 - k, 2, own_out)

    cot_pad = rimmed(cotangent, cot_edges)
    away = tap_sum(cot_pad, mix_far, n_rows, n_cols, True).astype(bf16)
    grad_hidden = tap_sum(cot_pad, mix_own, n_rows, n_cols, True)

    def taps_of(block):
        return block.reshape(n_rows, 2, n_cols, 2, own_in)

    near, far = taps_of(deep), taps_of(deep_far)
    preact = jnp.einsum("rawbc,abcd->drw", near, down_own, preferred_element_type=f32)
    preact = preact + jnp.einsum("rawbc,abcd->drw", far, down_far, preferred_element_type=f32)
    cdf = normal_cdf(preact)
    hidden = (preact * cdf).astype(bf16)
    hidden_far = flip(hidden, "chan", 1)
    own_edges, far_edges = edge_rows(hidden, False), edge_rows(hidden, True)
    hidden_far, away, down_far = lax.optimization_barrier((hidden_far, away, down_far))
    got = flip(away, "chan", 1)
    down_back = flip(down_far, "chan", 1)

    slope = cdf + preact * normal_pdf(preact)
    grad_pre = ((grad_hidden + got.astype(f32)) * slope).astype(bf16)
    grad_pre_far = flip(grad_pre, "chan", 1)

    def mix_terms(padded):
        terms = []
        for i in range(3):
            for j in range(3):
                window = padded[:, i : i + n_rows, j : j + n_cols]
                terms.append(
                    jnp.einsum("crw,drw->cd", window, cotangent, preferred_element_type=f32)
                )
        return jnp.stack(terms)

    own_pad = rimmed(hidden, own_edges)
    far_pad = rimmed(hidden_far, far_edges)
    grad_mix = reduce_halves(mix_terms(own_pad), mix_terms(far_pad), top) * scale
    grad_mix = grad_mix.transpose(1, 0, 2).reshape(-1, 3, 3, own_out)
    mixed = tap_sum(own_pad, mix_own, n_rows, n_cols, False)
    mixed = (mixed + tap_sum(far_pad, mix_far, n_rows, n_cols, False)).astype(bf16)

    def down_terms(patches):
        term = jnp.einsum("rawbc,drw->abcd", patches, grad_pre, preferred_element_type=f32)
        return term.reshape(4, own_in, own_out)

    grad_down, grad_pre_far = reduce_halves(
        down_terms(near), down_terms(far), top, grad_pre_far
    )
    grad_down = (grad_down * scale).transpose(1, 0, 2).reshape(-1, 2, 2, own_out)
    term = jnp.einsum("drw,abcd->crawb", grad_pre, down_own, preferred_element_type=f32)
    term = term + jnp.einsum(
        "drw,abcd->crawb", grad_pre_far, down_back, preferred_element_type=f32
    )
    return (mixed, grad_mix, grad_down, term.astype(bf16).reshape(image.shape))


def solution(mesh):
    sizes = dict(mesh.shape)
    n_tile = sizes["tile"]
    paired = sizes["chan"] == 2 and n_tile > 1 and n_tile & (n_tile - 1) == 0
    return jax.shard_map(
        pair_device if paired else per_device,
        mesh=mesh,
        in_specs=(
            P("chan", "tile", None),
            P(None, None, None, "chan"),
            P(None, None, None, "chan"),
            P("chan", "tile", None),
        ),
        out_specs=(
            P("chan", "tile", None),
            P("tile", None, None, "chan"),
            P("tile", None, None, "chan"),
            P("chan", "tile", None),
        ),
        check_vma=False,
    )
```
